32 devices in a mesh: row: 8 (over y, x, core), cls: 4 (over z).
Axes of the slice: x: 2, y: 2, z: 4, core: 2. Of those that a mesh axis runs over, the one named last changes fastest.
Arguments:
- hidden: bfloat16 [10240, 2048], P(('row', 'cls')), as said below
- labels: int32 [10240, 4], P('row'), may hold values from 0 to 4095
- weights: bfloat16 [2048, 4096], P('row', 'cls'), may hold values from -0.125 to 0.125
- bias: float32 [4096], P('cls'), may hold values from -3 to 1
- direction: bfloat16 [2048, 4096], P('row', 'cls'), may hold values from -6 to 6
Outputs:
- gradient: float32 [2048, 4096], P('row', 'cls')
- precond: float32 [2048, 4096], P('row', 'cls')
- hvp: float32 [2048, 4096], P('row', 'cls')
The draws below stay inside these ranges and needn't reach their ends.
Inputs may be any that keep to these rules, and one draw needn't show every extreme that they name: hidden states: entries independent up to an offset for each feature, with a positive scale for each context and for each feature.
All inputs are finite; a program needn't handle non-finite values.
Results may differ from the reference program's by a relative error of at most 0.0019.
Values may be sent and summed in bfloat16 or wider, within the bound.
A program may use at most 128 MiB of HBM per device.

```python
import math
import jax
import jax.numpy as jnp
from jax import lax

D = 2048
C = 4096
K = 4
TOK_DEV = 1280
TOKENS = 10240


def draw_hidden(key, part):
    key_base, key_rows, key_cols = jax.random.split(key, 3)
    base = jax.random.normal(key_base, (TOKENS, D), jnp.float32)
    row_scale = jnp.exp(jax.random.uniform(key_rows, (TOKENS, 1), jnp.float32, math.log(0.3), math.log(3.0)))
    col_scale = jnp.exp(jax.random.uniform(key_cols, (1, D), jnp.float32, math.log(0.3), math.log(3.0)))
    return (base * row_scale * col_scale).astype(jnp.bfloat16)


def place_ends(array, rng, low, high):
    longest = array.shape.index(max(array.shape))
    spots = []
    for shift in (0, 1):
        where = [jax.random.randint(jax.random.fold_in(rng, axis), (), 0, length) for axis, length in enumerate(array.shape)]
        where[longest] = (where[longest] + shift) % array.shape[longest]
        spots.append(tuple(where))
    return array.at[spots[0]].set(low).at[spots[1]].set(high)


def block_scale(rng, dims, shards, smallest, largest):
    loudness, own = 1.0, jax.random.fold_in(rng, 6)
    for position, parts in shards:
        heights = jnp.exp(jax.random.uniform(jax.random.fold_in(own, position), (parts,), jnp.float32, smallest / len(shards), largest / len(shards)))
        loudness = loudness * jnp.repeat(heights, dims[position] // parts).reshape([-1 if axis == position else 1 for axis in range(len(dims))])
    return loudness


def normal_values(own_key, extent, scale, bound, pieces=(), kind=jnp.bfloat16):
    loudness = block_scale(own_key, extent, pieces, -0.22, 0.18) if pieces else 1.0
    result = jax.random.normal(own_key, extent, jnp.float32) * scale * loudness
    return jnp.minimum(jnp.maximum(result, -bound), bound).astype(kind)


def setup_inputs(seed: int = 0) -> dict:
    key_list = jax.random.split(jax.random.key(seed), 6)
    hidden = draw_hidden(jax.random.fold_in(key_list[5], 71), 0)
    labels = place_ends(jax.random.randint(key_list[1], (TOKENS, K), 0, C), jax.random.fold_in(key_list[1], 1), 0, C - 1).astype(jnp.int32)
    weights = normal_values(key_list[2], (D, C), D ** -0.5, 0.125, ((0, 8), (1, 4)))
    bias = jnp.clip(-3.0 + 4.0 * jax.random.uniform(key_list[3], (C,), jnp.float32) ** block_scale(key_list[3], (C,), ((0, 4),), -0.2, 0.2), -3.0, 1.0)
    direction = normal_values(key_list[4], (D, C), 1.0, 6.0, ((0, 8), (1, 4)))
    return dict(hidden=hidden, labels=labels, weights=weights, bias=bias, direction=direction)


def reference(hidden, labels, weights, bias, direction):
    block_rows = TOK_DEV
    count = TOKENS // block_rows
    hidden_blocks = hidden.reshape(count, block_rows, D)
    label_blocks = labels.reshape(count, block_rows, K)
    class_ids = jnp.arange(C, dtype=jnp.int32)

    def accumulate(sums_in, inputs):
        block_h, block_l = inputs
        targets = jnp.any(block_l[:, :, None] == class_ids[None, None, :], axis=1).astype(jnp.float32)
        logits = jnp.dot(block_h, weights, preferred_element_type=jnp.float32) + bias[None, :]
        probs = jax.nn.sigmoid(logits)
        residual = (probs - targets).astype(jnp.bfloat16)
        curvature = probs * (1.0 - probs)
        curv_low = curvature.astype(jnp.bfloat16)
        squares = (block_h.astype(jnp.float32) * block_h.astype(jnp.float32)).astype(jnp.bfloat16)
        projected = jnp.dot(block_h, direction, preferred_element_type=jnp.float32)
        weighted = (curvature * projected).astype(jnp.bfloat16)
        grad_sum = sums_in[0] + jnp.dot(block_h.T, residual, preferred_element_type=jnp.float32)
        diag_sum = sums_in[1] + jnp.dot(squares.T, curv_low, preferred_element_type=jnp.float32)
        hvp_sum = sums_in[2] + jnp.dot(block_h.T, weighted, preferred_element_type=jnp.float32)
        return ((grad_sum, diag_sum, hvp_sum), None)
    zeros = jnp.zeros((D, C), jnp.float32)
    sums_out, unused = lax.scan(accumulate, (zeros, zeros, zeros), (hidden_blocks, label_blocks))
    row_count = jnp.float32(TOKENS)
    gradient = sums_out[0] / jnp.sqrt(row_count)
    precond = gradient / (sums_out[1] / row_count + 0.1)
    hvp = sums_out[2] / row_count
    return (gradient, precond, hvp)
```

```python
import functools
import math

import jax
import jax.numpy as jnp
from jax import lax
from jax.experimental import pallas as pl
from jax.experimental.pallas import tpu as pltpu
from jax.sharding import PartitionSpec as P

MESH = pl.DeviceIdType.MESH
F32 = jnp.float32
BF16 = jnp.bfloat16


def bits_of(mask):
    return [1 << i for i in range(mask.bit_length()) if (mask >> i) & 1]


def flip(r, mask):
    for b in bits_of(mask):
        r = r + b - 2 * b * lax.rem(lax.div(r, b), 2)
    return r


def first_of(mask, order):
    for i, b in enumerate(order):
        if mask & b:
            return i
    return len(order)


def kernel(R, Z, Q, lab, bias, hid, wts, dirn, g_out, p_out, v_out,
           H, WV, RHS, LT, TMP, CS, CR, SS, SR,
           loc_sem, w_send, w_recv, up_send, dn_send, h_recv,
           c_send, c_recv, s_send, s_recv):
    r = lax.axis_index("row")
    z = lax.axis_index("cls")
    T = hid.shape[0]
    D = hid.shape[1]
    F, C = wts.shape
    CH = C // 2
    TQ = T // Q
    ici = [1 << i for i in range(1, R.bit_length() - 1)]
    orders = (ici, ici[::-1])
    n = len(ici)
    masks = [2 * i for i in range(R // 2)]
    up, dn = lax.rem(z + 1, Z), lax.rem(z + Z - 1, Z)
    has_up, has_dn = z < Z - 1, z > 0

    def hrows(k, q):
        return pl.ds(pl.multiple_of(k * T + q * TQ, TQ), TQ)

    def frows(s):
        return pl.ds(pl.multiple_of(s * F, F), F)

    srcs = (wts, dirn)
    locals_ = [pltpu.make_async_copy(hid, H.at[pl.ds(pl.multiple_of(z * T, T), T), :], loc_sem.at[0])]
    for a in range(2):
        locals_.append(pltpu.make_async_copy(srcs[a], WV.at[a, frows(r), :], loc_sem.at[1 + a]))
    for c in locals_:
        c.start()

    barrier = pltpu.get_barrier_semaphore()
    for b in [1] + ici:
        pl.semaphore_signal(barrier, inc=1, device_id=(flip(r, b), z), device_id_type=MESH)

    @pl.when(has_up)
    def _():
        pl.semaphore_signal(barrier, inc=1, device_id=(r, up), device_id_type=MESH)

    @pl.when(has_dn)
    def _():
        pl.semaphore_signal(barrier, inc=1, device_id=(r, dn), device_id_type=MESH)

    pl.semaphore_wait(barrier, n + 1 + jnp.where(has_up, 1, 0) + jnp.where(has_dn, 1, 0))

    def h_copy(k, q, upward, own=False):
        rows = hrows(k, q)
        return pltpu.make_async_remote_copy(
            src_ref=hid.at[pl.ds(q * TQ, TQ), :] if own else H.at[rows, :],
            dst_ref=H.at[rows, :],
            send_sem=(up_send if upward else dn_send).at[k, q],
            recv_sem=h_recv.at[k, q],
            device_id=(r, up if upward else dn),
            device_id_type=MESH,
        )

    def h_own(q):
        @pl.when(has_up)
        def _():
            h_copy(z, q, True, own=True).start()

        @pl.when(has_dn)
        def _():
            h_copy(z, q, False, own=True).start()

    def h_pass(k, q, from_below):
        h_copy(k, q, from_below).wait_recv()

        @pl.when(has_up if from_below else has_dn)
        def _():
            h_copy(k, q, from_below).start()

    w_orders = (ici + [1], ici[::-1] + [1])
    w_started = []

    def w_copy(a, mask, to):
        rows = frows(flip(r, mask))
        return pltpu.make_async_remote_copy(
            src_ref=WV.at[a, rows, :] if mask else srcs[a],
            dst_ref=WV.at[a, rows, :],
            send_sem=w_send.at[a, (mask | to) - 1],
            recv_sem=w_recv.at[a, (mask | to) - 1],
            device_id=(flip(r, to), z),
            device_id_type=MESH,
        )

    def w_forward(a, mask):
        order = w_orders[a]
        after = max([order.index(b) for b in bits_of(mask)], default=-1)
        for b in order[after + 1:]:
            c = w_copy(a, mask, b)
            c.start()
            w_started.append(c)

    def w_wait(a, mask):
        rows = frows(flip(r, mask))
        pltpu.make_async_remote_copy(
            src_ref=WV.at[a, rows, :], dst_ref=WV.at[a, rows, :],
            send_sem=w_send.at[a, mask - 1], recv_sem=w_recv.at[a, mask - 1],
            device_id=(flip(r, 1), z), device_id_type=MESH,
        ).wait_recv()

    for a in range(2):
        w_forward(a, 0)
    for q in range(Q):
        h_own(q)

    def h_pass_one(q):
        @pl.when(has_dn)
        def _():
            h_pass(z - 1, q, True)

        @pl.when(has_up)
        def _():
            h_pass(z + 1, q, False)

    arrivals = sorted([m for m in masks if m], key=lambda m: (len(bits_of(m)), m))
    for pos, m in enumerate(arrivals):
        for a in range(2):
            mm = m if a == 0 else sum(ici[n - 1 - ici.index(b)] for b in bits_of(m))
            w_wait(a, mm)
            w_forward(a, mm)
        if pos >= len(arrivals) - Q:
            h_pass_one(pos - (len(arrivals) - Q))
    for c in locals_:
        c.wait()
    for a in range(2):
        for m in masks:
            w_wait(a, m | 1)

    CB = min(256, C)
    class0 = z * C

    def operands(k):
        rows = pl.ds(pl.multiple_of(k * T, T), T)
        labels = lab[rows, :]
        for j in range(C // CB):
            cols = pl.ds(j * CB, CB)
            x = H[rows, :]
            logits = jnp.dot(x, WV[0, :, cols], preferred_element_type=F32) + bias[:, cols]
            ids = class0 + j * CB + lax.broadcasted_iota(jnp.int32, (T, CB), 1)
            hit = labels[:, 0:1] == ids
            for i in range(1, labels.shape[1]):
                hit = hit | (labels[:, i:i + 1] == ids)
            probs = jax.nn.sigmoid(logits)
            curv = probs * (1.0 - probs)
            RHS[0, rows, cols] = (probs - jnp.where(hit, 1.0, 0.0)).astype(BF16)
            RHS[1, rows, cols] = curv.astype(BF16)
            proj = jnp.dot(x, WV[1, :, cols], preferred_element_type=F32)
            RHS[2, rows, cols] = (curv * proj).astype(BF16)

    def step(t, carry):
        d = lax.div(t + 1, 2)
        below = lax.rem(t, 2) == 1
        k = jnp.where(below, z - d, z + d)

        @pl.when(jnp.logical_and(k >= 0, k < Z))
        def _():
            @pl.when(jnp.logical_and(d > 1, below))
            def _():
                for q in range(Q):
                    h_pass(k, q, True)

            @pl.when(jnp.logical_and(d > 1, jnp.logical_not(below)))
            def _():
                for q in range(Q):
                    h_pass(k, q, False)

            operands(k)
        return carry

    lax.fori_loop(0, 2 * Z - 1, step, 0)

    FB = max(F, 128)

    def left(s):
        base = lax.div(s * F, FB) * FB
        h = H[:, pl.ds(pl.multiple_of(base, FB), FB)].T
        LT[0] = h
        h32 = h.astype(F32)
        LT[1] = (h32 * h32).astype(BF16)
        return s * F - base

    def partial(off, a, h):
        p = jnp.dot(LT[a % 2], RHS[a, :, pl.ds(h * CH, CH)], preferred_element_type=F32)
        if FB == F:
            return p
        TMP[...] = p
        return TMP[pl.ds(pl.multiple_of(off, F), F), :]

    started = []

    turn = sorted(masks, key=lambda m: (-len(bits_of(m)), m))
    core_copies = {}

    def c_copy(m, a):
        return pltpu.make_async_remote_copy(
            src_ref=CS.at[turn.index(m) % 2, a], dst_ref=CR.at[m // 2, a],
            send_sem=c_send.at[m // 2, a], recv_sem=c_recv.at[m // 2, a],
            device_id=(flip(r, 1), z), device_id_type=MESH,
        )

    def s_copy(h, m, a, to):
        i = m // 2 - 1
        return pltpu.make_async_remote_copy(
            src_ref=SS.at[h, i, a], dst_ref=SR.at[h, i, a],
            send_sem=s_send.at[h, i, a], recv_sem=s_recv.at[h, i, a],
            device_id=(flip(r, to), z), device_id_type=MESH,
        )

    def other(m):
        off = left(flip(r, m | 1))
        for a in range(3):
            at = turn.index(m)
            if at >= 2:
                core_copies.pop((turn[at - 2], a)).wait_send()
            for h in range(2):
                CS[at % 2, a, :, pl.ds(h * CH, CH)] = partial(off, a, h)
            core_copies[m, a] = c_copy(m, a)
            core_copies[m, a].start()

    def send_stage(h, m, a, value):
        SS[h, m // 2 - 1, a] = value.astype(BF16)
        c = s_copy(h, m, a, orders[h][first_of(m, orders[h])])
        c.start()
        started.append(c)

    def mine(m):
        off = left(flip(r, m))
        for a in range(3):
            c_copy(m, a).wait_recv()
            for h in range(2):
                t = partial(off, a, h) + CR[m // 2, a, :, pl.ds(h * CH, CH)]
                if first_of(m, orders[h]) == 0 and n:
                    send_stage(h, m, a, t)
                else:
                    CR[m // 2, a, :, pl.ds(h * CH, CH)] = t

    def gathered(h, m, a, upto):
        t = CR[m // 2, a, :, pl.ds(h * CH, CH)]
        for j in range(upto):
            src = m | orders[h][j]
            s_copy(h, src, a, orders[h][j]).wait_recv()
            t = t + SR[h, src // 2 - 1, a].astype(F32)
        return t

    other(turn[0])
    for i, m in enumerate(turn):
        if i + 1 < len(turn):
            other(turn[i + 1])
        mine(m)
    for i in range(1, n):
        for m in turn:
            for a in range(3):
                for h in range(2):
                    if m and first_of(m, orders[h]) == i:
                        send_stage(h, m, a, gathered(h, m, a, i))

    count = float(T * Z * R)
    for h in range(2):
        cols = pl.ds(h * CH, CH)
        grad = gathered(h, 0, 0, n) * (1.0 / math.sqrt(count))
        g_out[:, cols] = grad
        p_out[:, cols] = grad / (gathered(h, 0, 1, n) * (1.0 / count) + 0.1)
        v_out[:, cols] = gathered(h, 0, 2, n) * (1.0 / count)

    for c in w_started + started + list(core_copies.values()):
        c.wait_send()

    def drain(k, carry):
        for q in range(Q):
            @pl.when(jnp.logical_and(has_up, k <= z))
            def _():
                h_copy(k, q, True).wait_send()

            @pl.when(jnp.logical_and(has_dn, k >= z))
            def _():
                h_copy(k, q, False).wait_send()
        return carry

    lax.fori_loop(0, Z, drain, 0)


def body(R, Z, hidden, labels, weights, bias, direction):
    T, D = hidden.shape
    F, C = weights.shape
    Q = 2
    rows = T * Z
    FB = max(F, 128)
    n_masks = R // 2
    out = jax.ShapeDtypeStruct((F, C), F32)
    vmem = pl.BlockSpec(memory_space=pltpu.VMEM)
    hbm = pl.BlockSpec(memory_space=pl.ANY)
    dma = pltpu.SemaphoreType.DMA
    return pl.pallas_call(
        functools.partial(kernel, R, Z, Q),
        out_shape=(out, out, out),
        in_specs=[vmem, vmem, hbm, hbm, hbm],
        out_specs=(vmem, vmem, vmem),
        scratch_shapes=[
            pltpu.VMEM((rows, D), BF16),
            pltpu.VMEM((2, F * R, C), BF16),
            pltpu.VMEM((3, rows, C), BF16),
            pltpu.VMEM((2, FB, rows), BF16),
            pltpu.VMEM((FB, C // 2) if FB != F else (8, 128), F32),
            pltpu.VMEM((2, 3, F, C), F32),
            pltpu.VMEM((n_masks, 3, F, C), F32),
            pltpu.VMEM((2, n_masks - 1, 3, F, C // 2), BF16),
            pltpu.VMEM((2, n_masks - 1, 3, F, C // 2), BF16),
            dma((3,)),
            dma((2, R - 1)),
            dma((2, R - 1)),
            dma((Z, Q)),
            dma((Z, Q)),
            dma((Z, Q)),
            dma((n_masks, 3)),
            dma((n_masks, 3)),
            dma((2, n_masks - 1, 3)),
            dma((2, n_masks - 1, 3)),
        ],
        compiler_params=pltpu.CompilerParams(
            collective_id=0, has_side_effects=True, vmem_limit_bytes=62 * 1024 * 1024
        ),
        cost_estimate=pl.CostEstimate(
            flops=10 * rows * D * C, bytes_accessed=2 * T * D + 4 * F * C + 12 * F * C,
            transcendentals=rows * C,
        ),
    )(labels, bias.reshape(1, C), hidden, weights, direction)


def solution(mesh):
    return jax.shard_map(
        functools.partial(body, mesh.shape["row"], mesh.shape["cls"]),
        mesh=mesh,
        in_specs=(
            P(("row", "cls"), None),
            P("row", None),
            P("row", "cls"),
            P("cls"),
            P("row", "cls"),
        ),
        out_specs=(P("row", "cls"), P("row", "cls"), P("row", "cls")),
        check_vma=False,
    )
```

```python
import functools
import math

import jax
import jax.numpy as jnp
from jax import lax
from jax.experimental import pallas as pl
from jax.experimental.pallas import tpu as pltpu
from jax.sharding import PartitionSpec as P

MESH = pl.DeviceIdType.MESH
F32 = jnp.float32
BF16 = jnp.bfloat16


def bits_of(mask):
    return [1 << i for i in range(mask.bit_length()) if (mask >> i) & 1]


def flip(r, mask):
    for b in bits_of(mask):
        r = r + b - 2 * b * lax.rem(lax.div(r, b), 2)
    return r


def first_of(mask, order):
    for i, b in enumerate(order):
        if mask & b:
            return i
    return len(order)


def kernel(R, Z, Q, lab, bias, hid, wts, dirn, sums_out,
           H, WV, RHS, LT, TMP, CS, CR, SS, SR, LAB,
           loc_sem, w_send, w_recv, up_send, dn_send, h_recv,
           c_send, c_recv, s_send, s_recv):
    r = lax.axis_index("row")
    z = lax.axis_index("cls")
    T = hid.shape[0]
    D = hid.shape[1]
    F, C = wts.shape
    CH = C // 2
    TQ = T // Q
    ici = [1 << i for i in range(1, R.bit_length() - 1)]
    orders = (ici, ici[::-1])
    n = len(ici)
    masks = [2 * i for i in range(R // 2)]
    up, dn = lax.rem(z + 1, Z), lax.rem(z + Z - 1, Z)
    has_up, has_dn = z < Z - 1, z > 0

    def hrows(k, q):
        return pl.ds(pl.multiple_of(k * T + q * TQ, TQ), TQ)

    def frows(s):
        return pl.ds(pl.multiple_of(s * F, F), F)

    srcs = (wts, dirn)
    locals_ = [pltpu.make_async_copy(hid, H.at[pl.ds(pl.multiple_of(z * T, T), T), :], loc_sem.at[0])]
    for a in range(2):
        locals_.append(pltpu.make_async_copy(srcs[a], WV.at[a, frows(r), :], loc_sem.at[1 + a]))
    for c in locals_:
        c.start()

    barrier = pltpu.get_barrier_semaphore()
    for b in [1] + ici:
        pl.semaphore_signal(barrier, inc=1, device_id=(flip(r, b), z), device_id_type=MESH)

    @pl.when(has_up)
    def _():
        pl.semaphore_signal(barrier, inc=1, device_id=(r, up), device_id_type=MESH)

    @pl.when(has_dn)
    def _():
        pl.semaphore_signal(barrier, inc=1, device_id=(r, dn), device_id_type=MESH)

    pl.semaphore_wait(barrier, n + 1 + jnp.where(has_up, 1, 0) + jnp.where(has_dn, 1, 0))

    def h_copy(k, q, upward, own=False):
        rows = hrows(k, q)
        return pltpu.make_async_remote_copy(
            src_ref=hid.at[pl.ds(q * TQ, TQ), :] if own else H.at[rows, :],
            dst_ref=H.at[rows, :],
            send_sem=(up_send if upward else dn_send).at[k, q],
            recv_sem=h_recv.at[k, q],
            device_id=(r, up if upward else dn),
            device_id_type=MESH,
        )

    def h_own(q):
        @pl.when(has_up)
        def _():
            h_copy(z, q, True, own=True).start()

        @pl.when(has_dn)
        def _():
            h_copy(z, q, False, own=True).start()

    def h_pass(k, q, from_below):
        h_copy(k, q, from_below).wait_recv()

        @pl.when(has_up if from_below else has_dn)
        def _():
            h_copy(k, q, from_below).start()

    w_orders = (ici + [1], ici[::-1] + [1])
    w_started = []

    def w_copy(a, mask, to):
        rows = frows(flip(r, mask))
        return pltpu.make_async_remote_copy(
            src_ref=WV.at[a, rows, :] if mask else srcs[a],
            dst_ref=WV.at[a, rows, :],
            send_sem=w_send.at[a, (mask | to) - 1],
            recv_sem=w_recv.at[a, (mask | to) - 1],
            device_id=(flip(r, to), z),
            device_id_type=MESH,
        )

    def w_forward(a, mask):
        order = w_orders[a]
        after = max([order.index(b) for b in bits_of(mask)], default=-1)
        for b in order[after + 1:]:
            c = w_copy(a, mask, b)
            c.start()
            w_started.append(c)

    def w_wait(a, mask):
        rows = frows(flip(r, mask))
        pltpu.make_async_remote_copy(
            src_ref=WV.at[a, rows, :], dst_ref=WV.at[a, rows, :],
            send_sem=w_send.at[a, mask - 1], recv_sem=w_recv.at[a, mask - 1],
            device_id=(flip(r, 1), z), device_id_type=MESH,
        ).wait_recv()

    for a in range(2):
        w_forward(a, 0)
    for q in range(Q):
        h_own(q)
    LAB[...] = lab[...].T

    def h_pass_one(q):
        @pl.when(has_dn)
        def _():
            h_pass(z - 1, q, True)

        @pl.when(has_up)
        def _():
            h_pass(z + 1, q, False)

    arrivals = sorted([m for m in masks if m], key=lambda m: (len(bits_of(m)), m))
    def w_pass(some):
        for m in some:
            for a in range(2):
                mm = m if a == 0 else sum(ici[n - 1 - ici.index(b)] for b in bits_of(m))
                w_wait(a, mm)
                w_forward(a, mm)

    w_pass(arrivals[:n])
    for q in range(Q):
        h_pass_one(q)
    w_pass(arrivals[n:])
    for c in locals_:
        c.wait()
    for a in range(2):
        for m in masks:
            w_wait(a, m | 1)

    CB = min(256, C)
    class0 = z * C

    def operands(k):
        rows = pl.ds(pl.multiple_of(k * T, T), T)
        labels = LAB[rows, :]
        for j in range(C // CB):
            cols = pl.ds(j * CB, CB)
            x = H[rows, :]
            logits = jnp.dot(x, WV[0, :, cols], preferred_element_type=F32) + bias[:, cols]
            ids = class0 + j * CB + lax.broadcasted_iota(jnp.int32, (T, CB), 1)
            hit = labels[:, 0:1] == ids
            for i in range(1, labels.shape[1]):
                hit = hit | (labels[:, i:i + 1] == ids)
            probs = jax.nn.sigmoid(logits)
            curv = probs * (1.0 - probs)
            RHS[0, rows, cols] = (probs - jnp.where(hit, 1.0, 0.0)).astype(BF16)
            RHS[1, rows, cols] = curv.astype(BF16)
            proj = jnp.dot(x, WV[1, :, cols], preferred_element_type=F32)
            RHS[2, rows, cols] = (curv * proj).astype(BF16)

    def step(t, carry):
        d = lax.div(t + 1, 2)
        below = lax.rem(t, 2) == 1
        k = jnp.where(below, z - d, z + d)

        @pl.when(jnp.logical_and(k >= 0, k < Z))
        def _():
            @pl.when(jnp.logical_and(d > 1, below))
            def _():
                for q in range(Q):
                    h_pass(k, q, True)

            @pl.when(jnp.logical_and(d > 1, jnp.logical_not(below)))
            def _():
                for q in range(Q):
                    h_pass(k, q, False)

            operands(k)
        return carry

    lax.fori_loop(0, 2 * Z - 1, step, 0)

    FB = max(F, 128)

    def left(s):
        base = lax.div(s * F, FB) * FB
        h = H[:, pl.ds(pl.multiple_of(base, FB), FB)].T
        LT[0] = h
        h32 = h.astype(F32)
        LT[1] = (h32 * h32).astype(BF16)
        return s * F - base

    def partial(off, a, h):
        p = jnp.dot(LT[a % 2], RHS[a, :, pl.ds(h * CH, CH)], preferred_element_type=F32)
        if FB == F:
            return p
        TMP[...] = p
        return TMP[pl.ds(pl.multiple_of(off, F), F), :]

    started = []

    turn = sorted(masks, key=lambda m: (-len(bits_of(m)), m))
    core_copies = {}

    def c_copy(m, a):
        return pltpu.make_async_remote_copy(
            src_ref=CS.at[turn.index(m) % 2, a], dst_ref=CR.at[m // 2, a],
            send_sem=c_send.at[m // 2, a], recv_sem=c_recv.at[m // 2, a],
            device_id=(flip(r, 1), z), device_id_type=MESH,
        )

    def s_copy(h, m, a, to):
        i = m // 2 - 1
        return pltpu.make_async_remote_copy(
            src_ref=SS.at[h, i, a], dst_ref=SR.at[h, i, a],
            send_sem=s_send.at[h, i, a], recv_sem=s_recv.at[h, i, a],
            device_id=(flip(r, to), z), device_id_type=MESH,
        )

    def other(m):
        off = left(flip(r, m | 1))
        for a in range(3):
            at = turn.index(m)
            if at >= 2:
                core_copies.pop((turn[at - 2], a)).wait_send()
            for h in range(2):
                CS[at % 2, a, :, pl.ds(h * CH, CH)] = partial(off, a, h)
            core_copies[m, a] = c_copy(m, a)
            core_copies[m, a].start()

    def send_stage(h, m, a, value):
        SS[h, m // 2 - 1, a] = value.astype(BF16)
        c = s_copy(h, m, a, orders[h][first_of(m, orders[h])])
        c.start()
        started.append(c)

    def mine(m):
        off = left(flip(r, m))
        for a in range(3):
            c_copy(m, a).wait_recv()
            for h in range(2):
                t = partial(off, a, h) + CR[m // 2, a, :, pl.ds(h * CH, CH)]
                if first_of(m, orders[h]) == 0 and n:
                    send_stage(h, m, a, t)
                else:
                    CR[m // 2, a, :, pl.ds(h * CH, CH)] = t

    def gathered(h, m, a, upto):
        t = CR[m // 2, a, :, pl.ds(h * CH, CH)]
        for j in range(upto):
            src = m | orders[h][j]
            s_copy(h, src, a, orders[h][j]).wait_recv()
            t = t + SR[h, src // 2 - 1, a].astype(F32)
        return t

    ahead = turn[:-1]
    other(ahead[0])
    for i, m in enumerate(ahead):
        if i + 1 < len(ahead):
            other(ahead[i + 1])
        mine(m)
    other(turn[-1])
    mine(turn[-1])
    for i in range(1, n):
        for m in turn:
            for a in range(3):
                for h in range(2):
                    if m and first_of(m, orders[h]) == i:
                        send_stage(h, m, a, gathered(h, m, a, i))

    for a in range(3):
        for h in range(2):
            sums_out[a, :, pl.ds(h * CH, CH)] = gathered(h, 0, a, n)

    for c in w_started + started + list(core_copies.values()):
        c.wait_send()

    def drain(k, carry):
        for q in range(Q):
            @pl.when(jnp.logical_and(has_up, k <= z))
            def _():
                h_copy(k, q, True).wait_send()

            @pl.when(jnp.logical_and(has_dn, k >= z))
            def _():
                h_copy(k, q, False).wait_send()
        return carry

    lax.fori_loop(0, Z, drain, 0)


def body(R, Z, hidden, labels, weights, bias, direction):
    T, D = hidden.shape
    F, C = weights.shape
    Q = 2
    rows = T * Z
    FB = max(F, 128)
    n_masks = R // 2
    vmem = pl.BlockSpec(memory_space=pltpu.VMEM)
    hbm = pl.BlockSpec(memory_space=pl.ANY)
    dma = pltpu.SemaphoreType.DMA
    sums = pl.pallas_call(
        functools.partial(kernel, R, Z, Q),
        out_shape=jax.ShapeDtypeStruct((3, F, C), F32),
        in_specs=[vmem, vmem, hbm, hbm, hbm],
        out_specs=vmem,
        scratch_shapes=[
            pltpu.VMEM((rows, D), BF16),
            pltpu.VMEM((2, F * R, C), BF16),
            pltpu.VMEM((3, rows, C), BF16),
            pltpu.VMEM((2, FB, rows), BF16),
            pltpu.VMEM((FB, C // 2) if FB != F else (8, 128), F32),
            pltpu.VMEM((2, 3, F, C), F32),
            pltpu.VMEM((n_masks, 3, F, C), F32),
            pltpu.VMEM((2, n_masks - 1, 3, F, C // 2), BF16),
            pltpu.VMEM((2, n_masks - 1, 3, F, C // 2), BF16),
            pltpu.VMEM((rows, labels.shape[1]), jnp.int32),
            dma((3,)),
            dma((2, R - 1)),
            dma((2, R - 1)),
            dma((Z, Q)),
            dma((Z, Q)),
            dma((Z, Q)),
            dma((n_masks, 3)),
            dma((n_masks, 3)),
            dma((2, n_masks - 1, 3)),
            dma((2, n_masks - 1, 3)),
        ],
        compiler_params=pltpu.CompilerParams(
            collective_id=0, has_side_effects=True, vmem_limit_bytes=62 * 1024 * 1024
        ),
        cost_estimate=pl.CostEstimate(
            flops=10 * rows * D * C, bytes_accessed=2 * T * D + 4 * F * C + 12 * F * C,
            transcendentals=rows * C,
        ),
    )(labels.T, bias.reshape(1, C), hidden, weights, direction)
    count = float(rows * R)
    gradient = sums[0] * (1.0 / math.sqrt(count))
    precond = gradient / (sums[1] * (1.0 / count) + 0.1)
    return gradient, precond, sums[2] * (1.0 / count)


def solution(mesh):
    return jax.shard_map(
        functools.partial(body, mesh.shape["row"], mesh.shape["cls"]),
        mesh=mesh,
        in_specs=(
            P(("row", "cls"), None),
            P("row", None),
            P("row", "cls"),
            P("cls"),
            P("row", "cls"),
        ),
        out_specs=(P("row", "cls"), P("row", "cls"), P("row", "cls")),
        check_vma=False,
    )
```
